32 devices in a mesh: scan: 2 (over y), wide: 8 (over z, x), narrow: 2 (over core).
Axes of the slice: x: 2, y: 2, z: 4, core: 2. Of those that a mesh axis runs over, the one named last changes fastest.
Arguments:
- projections: float32 [32, 512, 512], P(('scan', 'wide', 'narrow')), parts along dimension 0, may hold values from 0.2 to 1
- angle_index: int32 [32], P('scan'), parts along dimension 0, may hold values from 0 to 15, each once
Outputs:
- volume: float32 [1024, 64, 128], P(('scan', 'wide'), 'narrow'), parts along dimension 0
The draws below stay inside these ranges and needn't reach their ends.
There are 2 independent parts, one for each index of `scan`. The reference program is written for one: setup_inputs(seed, part) draws one part's arguments, and reference() takes and returns one part's arrays. A program takes and returns all parts, laid end to end along the dimension named above; each array names one. Nothing has to cross between parts.
Inputs may be any that keep to these rules, and one draw needn't show every extreme that they name: `angle_index`: each angle number appears exactly once.
All inputs are finite; a program needn't handle non-finite values.
Results may differ from the reference program's by a relative error of at most 0.0003.
Values sent between devices are 32-bit elements; how exact they have to be, the bound alone decides.
A program may use at most 192 MiB of HBM per device.

```python
import math
import jax
import jax.numpy as jnp
from jax import lax

ROWS = 512
COLS = 512
XV = 128
YV = 64
STEPS = 4
ANGLES = 16


def block_levels(own_key, dims, cuts, least, top_value):
    def one(dim, parts):
        heights = jax.random.uniform(jax.random.fold_in(jax.random.fold_in(own_key, 6), dim), (parts,), jnp.float32, least / len(cuts), top_value / len(cuts))
        return jnp.repeat(jnp.exp(heights), dims[dim] // parts).reshape((-1,) + (1,) * (len(dims) - dim - 1))

    gain = one(*cuts[0])
    for cut in cuts[1:]:
        gain = gain * one(*cut)
    return gain


def setup_inputs(seed: int = 0, part: int = 0) -> dict:
    arg_keys = jax.random.split(jax.random.key(seed), 3)
    own_keys = jax.random.split(jax.random.fold_in(arg_keys[2], part), 3)
    return {
        "projections": jnp.clip(0.2 + 0.8 * jax.random.uniform(own_keys[0], (ANGLES, ROWS, COLS), jnp.float32) ** block_levels(own_keys[0], (ANGLES, ROWS, COLS), ((0, 16),), -0.2, 0.2), 0.2, 1.0),
        "angle_index": jax.random.permutation(own_keys[1], ANGLES).astype(jnp.int32),
    }


paganin_strength = 0.25
attenuation = 0.01
contrast = 0.8
time_step = 0.15
highest = lax.Precision.HIGHEST


def paganin_symbol(row_count, col_count):
    row_sin = jnp.sin(jnp.arange(row_count, dtype=jnp.float32) * (math.pi / row_count))
    col_sin = jnp.sin(jnp.arange(col_count, dtype=jnp.float32) * (math.pi / col_count))
    spectral = 4.0 * row_sin[:, None] ** 2 + 4.0 * col_sin[None, :] ** 2
    return 1.0 / (1.0 + paganin_strength * spectral)


def ramp_kernel(col_count):
    grid_ints = jnp.arange(col_count, dtype=jnp.int32)
    offset = grid_ints[:, None] - grid_ints[None, :]
    is_odd = (offset % 2) != 0
    safe_dist = jnp.where(is_odd, offset.astype(jnp.float32), jnp.float32(1.0))
    odd_value = -1.0 / (math.pi * safe_dist) ** 2
    return jnp.where(offset == 0, jnp.float32(0.25), jnp.where(is_odd, odd_value, jnp.float32(0.0)))


def conduct(diff):
    return diff / (1.0 + (diff / contrast) ** 2)


def reference(projections, angle_index):
    total_angles = projections.shape[0]
    symbol = paganin_symbol(ROWS, COLS)
    kernel = ramp_kernel(COLS)

    def filter_one(projection):
        spectrum = jnp.fft.fft2(projection)
        smooth = jnp.real(jnp.fft.ifft2(spectrum * symbol))
        thickness = -jnp.log(smooth) / attenuation
        return jnp.dot(thickness, kernel, precision=highest, preferred_element_type=jnp.float32)

    filtered = lax.map(filter_one, projections)
    thetas = angle_index.astype(jnp.float32) * (math.pi / total_angles)
    x_coords = jnp.arange(XV, dtype=jnp.float32) - 0.5 * XV + 0.5
    y_coords = jnp.arange(YV, dtype=jnp.float32) - 0.5 * YV + 0.5

    def add_angle(accum, pair):
        sinogram, theta = pair
        position = jnp.cos(theta) * x_coords[None, :] + jnp.sin(theta) * y_coords[:, None] + (0.5 * COLS - 0.5)
        lower_pos = jnp.floor(position)
        fraction = position - lower_pos
        lower_index = lower_pos.astype(jnp.int32).reshape(-1)
        left_vals = jnp.take(sinogram, lower_index, axis=1).reshape(ROWS, YV, XV)
        right_vals = jnp.take(sinogram, lower_index + 1, axis=1).reshape(ROWS, YV, XV)
        return accum + (1.0 - fraction)[None] * left_vals + fraction[None] * right_vals, None

    start_sum = jnp.zeros((ROWS, YV, XV), jnp.float32)
    accum, unused_out = lax.scan(add_angle, start_sum, (filtered, thetas))
    current = accum * (math.pi / total_angles)
    for sweep_index in range(STEPS):
        padded = jnp.pad(current, 1, mode="edge")
        centre = padded[1:-1, 1:-1, 1:-1]
        update = conduct(padded[2:, 1:-1, 1:-1] - centre) + conduct(padded[:-2, 1:-1, 1:-1] - centre)
        update = update + conduct(padded[1:-1, 2:, 1:-1] - centre) + conduct(padded[1:-1, :-2, 1:-1] - centre)
        update = update + conduct(padded[1:-1, 1:-1, 2:] - centre) + conduct(padded[1:-1, 1:-1, :-2] - centre)
        current = centre + time_step * update
    return current
```

```python
import functools
import math

import jax
import jax.numpy as jnp
import ml_dtypes
import numpy as np
from jax import lax
from jax.experimental import pallas as pl
from jax.experimental.pallas import tpu as pltpu
from jax.sharding import PartitionSpec as P

XV = 128
YV = 64
STEPS = 4
GROUP = 16
MAIN = 128
SIDE = 8

paganin_strength = 0.25
attenuation = 0.01
contrast = 0.8
time_step = 0.15
bf16 = jnp.bfloat16
f32 = jnp.float32


def halves(table):
    high = table.astype(ml_dtypes.bfloat16)
    low = (table - high.astype(np.float64)).astype(ml_dtypes.bfloat16)
    return high, low


def hartley_table(count):
    grid = np.arange(count)
    phase = (grid[:, None] * grid[None, :] % count) * (2.0 * math.pi / count)
    return (np.cos(phase) + np.sin(phase)) / math.sqrt(count)


def window_columns(col_count):
    first = col_count // 2 - MAIN // 2
    middle = np.arange(first, first + MAIN)
    before = np.arange(first - SIDE, first)
    after = np.arange(first + MAIN, first + MAIN + SIDE)
    return np.concatenate([middle, before, after])


def ramp_table(col_count, scale):
    grid = np.arange(col_count)
    columns = window_columns(col_count)
    offset = grid[:, None] - columns[None, :]
    odd = offset % 2 != 0
    safe = np.where(odd, offset, 1)
    table = np.where(offset == 0, 0.25, np.where(odd, -1.0 / (math.pi * safe) ** 2, 0.0)) * scale
    return np.pad(table, ((0, 0), (0, 2 * MAIN - columns.size)))


def split(value):
    high = value.astype(bf16)
    return high, (value - high.astype(f32)).astype(bf16)


def dot3(left, right):
    dot = functools.partial(jnp.dot, preferred_element_type=f32)
    return dot(left[0], right[0]) + (dot(left[0], right[1]) + dot(left[1], right[0]))


def filter_kernel(x_ref, hh_ref, hl_ref, kh_ref, kl_ref, row_ref, col_ref, out_ref, ah, al, bh, bl):
    rows, cols = x_ref.shape
    block = 128

    def columns_first(step, carry):
        own = pl.ds(pl.multiple_of(step * block, block), block)
        part = dot3(split(x_ref[own, :]), (hh_ref[...], hl_ref[...]))
        ah[own, :], al[own, :] = split(part)
        return carry

    def damp(step, carry):
        own = pl.ds(pl.multiple_of(step * block, block), block)
        part = dot3((hh_ref[own, :], hl_ref[own, :]), (ah[...], al[...]))
        part = part / (row_ref[own, :] + col_ref[...])
        part = dot3(split(part), (hh_ref[...], hl_ref[...]))
        bh[own, :], bl[own, :] = split(part)
        return carry

    def ramp(step, carry):
        own = pl.ds(pl.multiple_of(step * block, block), block)
        part = dot3((hh_ref[own, :], hl_ref[own, :]), (bh[...], bl[...]))
        out_ref[own, :] = dot3(split(jnp.log(part)), (kh_ref[...], kl_ref[...]))
        return carry

    lax.fori_loop(0, rows // block, columns_first, 0)
    lax.fori_loop(0, rows // block, damp, 0)
    lax.fori_loop(0, rows // block, ramp, 0)


def filtered_window(projection, total_angles):
    rows, cols = projection.shape
    tables = halves(hartley_table(rows)) + halves(
        ramp_table(cols, -math.pi / (attenuation * total_angles))
    )
    row_part = 1.0 + paganin_strength * 4.0 * np.sin(np.pi * np.arange(rows) / rows) ** 2
    col_part = paganin_strength * 4.0 * np.sin(np.pi * np.arange(cols) / cols) ** 2
    vmem = pl.BlockSpec(memory_space=pltpu.VMEM)
    return pl.pallas_call(
        filter_kernel,
        out_shape=jax.ShapeDtypeStruct((rows, 2 * MAIN), f32),
        in_specs=[vmem] * 7,
        out_specs=vmem,
        scratch_shapes=[pltpu.VMEM((rows, cols), bf16)] * 4,
        compiler_params=pltpu.CompilerParams(vmem_limit_bytes=48 * 2**20),
        name="filter_window",
    )(
        projection,
        *[jnp.asarray(table) for table in tables],
        jnp.asarray(row_part[:, None].astype(np.float32)),
        jnp.asarray(col_part[None, :].astype(np.float32)),
    )


def conduct(diff):
    base = 1.0 + diff * diff * (1.0 / contrast**2)
    guess = pl.reciprocal(base, approx=True)
    return diff * (guess * (2.0 - base * guess))


def volume_kernel(plan, ang_ref, cos_ref, sin_ref, sino_ref, out_ref, f2, wh0, wl0, wh1, wl1, u):
    slab, tile_y, local_y, z_start, wide_count = plan
    total, depth = sino_ref.shape[0], sino_ref.shape[1]
    wide_pos, narrow_pos = lax.axis_index("wide"), lax.axis_index("narrow")
    y_skip = tile_y - (local_y - tile_y)
    y_first = narrow_pos * y_skip
    x_row = lax.broadcasted_iota(jnp.int32, (16, XV), 1).astype(f32) + (0.5 - 0.5 * XV)
    lanes16 = lax.broadcasted_iota(jnp.int32, (16, XV), 0)
    middle = [(lanes16 + (SIDE + 16 * j)).astype(f32).astype(bf16) for j in range(MAIN // 16)]
    outer = jnp.where(lanes16 < SIDE, lanes16, lanes16 + MAIN).astype(f32).astype(bf16)
    cells = middle + [outer]
    centre = 0.5 * MAIN + SIDE - 0.5

    def weights(group, pair, high_ref, low_ref):
        for side in range(2):
            own = slice(side * XV, (side + 1) * XV)
            y_pos = (y_first + 2 * pair + side).astype(f32) + (0.5 - 0.5 * YV)
            for a in range(GROUP):
                number = ang_ref[group * GROUP + a]
                place = x_row * cos_ref[number] + (y_pos * sin_ref[number] + centre)
                lower = jnp.floor(place)
                frac = place - lower
                coarse = jnp.floor(frac * 256.0 + 0.5) * (1.0 / 256.0)
                fine = frac - coarse
                here, there = lower.astype(bf16), (lower + 1.0).astype(bf16)
                left, right = (1.0 - coarse).astype(bf16), coarse.astype(bf16)
                left_fine, right_fine = (-fine).astype(bf16), fine.astype(bf16)
                zero = jnp.zeros_like(left)
                for j, cell in enumerate(cells):
                    row = a * MAIN + j * 16 if j < len(middle) else GROUP * MAIN + a * 16
                    is_here, is_there = cell == here, cell == there
                    high_ref[row : row + 16, own] = jnp.where(
                        is_here, left, jnp.where(is_there, right, zero)
                    )
                    low_ref[row : row + 16, own] = jnp.where(
                        is_here, left_fine, jnp.where(is_there, right_fine, zero)
                    )

    def project(group, pair, high_ref, low_ref):
        both = jnp.dot(f2[...], high_ref[...], preferred_element_type=f32)
        rest = jnp.dot(f2[:depth, :], low_ref[...], preferred_element_type=f32)
        value = both[:depth] + (both[depth:] + rest)
        for side in range(2):
            own = value[:, side * XV : (side + 1) * XV]
            if total > GROUP:
                own = own + jnp.where(group > 0, u[2 * pair + side], 0.0)
            u[2 * pair + side] = own

    def one_group(group, carry):
        for a in range(GROUP):
            high, low = split(sino_ref[group * GROUP + a])
            f2[:depth, a * MAIN : (a + 1) * MAIN] = high[:, :MAIN]
            f2[depth:, a * MAIN : (a + 1) * MAIN] = low[:, :MAIN]
        for half in range(2):
            parts = [
                sino_ref[group * GROUP + half * 8 + a][:, MAIN : MAIN + 2 * SIDE] for a in range(8)
            ]
            high, low = split(jnp.concatenate(parts, axis=1))
            own = slice(GROUP * MAIN + half * MAIN, GROUP * MAIN + (half + 1) * MAIN)
            f2[:depth, own] = high
            f2[depth:, own] = low
        weights(group, jnp.int32(0), wh0, wl0)

        def two_pairs(step, inner):
            weights(group, 2 * step + 1, wh1, wl1)
            project(group, 2 * step, wh0, wl0)
            weights(group, 2 * step + 2, wh0, wl0)
            project(group, 2 * step + 1, wh1, wl1)
            return inner

        lax.fori_loop(0, local_y // 4, two_pairs, 0)
        return carry

    if total > GROUP:
        lax.fori_loop(0, total // GROUP, one_group, 0)
    else:
        one_group(0, 0)

    z_ids = lax.broadcasted_iota(jnp.int32, (depth, XV), 0)
    x_ids = lax.broadcasted_iota(jnp.int32, (depth, XV), 1)
    has_z = z_ids < depth - 1
    has_x = x_ids < XV - 1

    def row_step(y, carry):
        now, flux_before = carry
        later = u[jnp.minimum(y + 1, local_y - 1)]
        flux_y = conduct(later - now)
        flux_z = conduct(jnp.where(has_z, pltpu.roll(now, depth - 1, 0) - now, 0.0))
        flux_x = conduct(jnp.where(has_x, pltpu.roll(now, XV - 1, 1) - now, 0.0))
        update = (flux_y - flux_before) + (flux_z - pltpu.roll(flux_z, 1, 0))
        update = update + (flux_x - pltpu.roll(flux_x, 1, 1))
        u[y] = now + time_step * update
        return later, flux_y

    for step in range(STEPS):
        lax.fori_loop(0, local_y, row_step, (u[0], jnp.zeros((depth, XV), f32)), unroll=2)

    z_skip = wide_pos * slab - z_start(wide_pos)
    if slab % 8 == 0:
        z_skip = pl.multiple_of(z_skip, 8)
    y_own = narrow_pos * (local_y - tile_y)
    for y in range(tile_y):
        out_ref[:, y, :] = u[y_own + y, pl.ds(z_skip, slab), :]


def shards(projections, angle_index):
    wide_count = lax.axis_size("wide")
    narrow_count = lax.axis_size("narrow")
    rows = projections.shape[1]
    per_device = projections.shape[0]
    total = angle_index.shape[0]
    slab = rows // wide_count
    depth = -(-(slab + 12) // 16) * 16
    tile_y = YV // narrow_count
    local_y = tile_y + STEPS

    def z_start(wide_pos):
        first = (wide_pos * slab + 8 - STEPS) // 8 * 8 - 8
        if isinstance(wide_pos, int):
            return min(max(first, 0), rows - depth)
        return jnp.minimum(jnp.maximum(first, 0), rows - depth)

    windows = [filtered_window(projections[i], total) for i in range(per_device)]
    window = jnp.stack(windows)
    slabs = jnp.stack(
        [window[:, z_start(w) : z_start(w) + depth] for w in range(wide_count) for n in range(narrow_count)]
    )
    sino = lax.all_to_all(slabs, ("wide", "narrow"), split_axis=0, concat_axis=0, tiled=True)
    sino = sino.reshape(total, depth, 2 * MAIN)
    angles = np.arange(total) * (math.pi / total)
    vmem = pl.BlockSpec(memory_space=pltpu.VMEM)
    smem = pl.BlockSpec(memory_space=pltpu.SMEM)
    inner = GROUP * (MAIN + 2 * SIDE)
    return pl.pallas_call(
        functools.partial(volume_kernel, (slab, tile_y, local_y, z_start, wide_count)),
        out_shape=jax.ShapeDtypeStruct((slab, tile_y, XV), f32),
        in_specs=[smem, smem, smem, vmem],
        out_specs=vmem,
        scratch_shapes=[pltpu.VMEM((2 * depth, inner), bf16)]
        + [pltpu.VMEM((inner, 2 * XV), bf16)] * 4
        + [pltpu.VMEM((local_y, depth, XV), f32)],
        compiler_params=pltpu.CompilerParams(vmem_limit_bytes=48 * 2**20),
        name="volume",
    )(
        angle_index,
        jnp.asarray(np.cos(angles).astype(np.float32)),
        jnp.asarray(np.sin(angles).astype(np.float32)),
        sino,
    )


def solution(mesh):
    return jax.shard_map(
        shards,
        mesh=mesh,
        in_specs=(P(("scan", "wide", "narrow"), None, None), P("scan")),
        out_specs=P(("scan", "wide"), "narrow", None),
        check_vma=False,
    )
```

```python
import functools
import math

import jax
import jax.numpy as jnp
import ml_dtypes
import numpy as np
from jax import lax
from jax.experimental import pallas as pl
from jax.experimental.pallas import tpu as pltpu
from jax.sharding import PartitionSpec as P

XV = 128
YV = 64
STEPS = 4
GROUP = 16
MAIN = 128
SIDE = 8

paganin_strength = 0.25
attenuation = 0.01
contrast = 0.8
time_step = 0.15
bf16 = jnp.bfloat16
f32 = jnp.float32


def halves(table):
    high = table.astype(ml_dtypes.bfloat16)
    low = (table - high.astype(np.float64)).astype(ml_dtypes.bfloat16)
    return high, low


def hartley_table(count):
    grid = np.arange(count)
    phase = (grid[:, None] * grid[None, :] % count) * (2.0 * math.pi / count)
    return (np.cos(phase) + np.sin(phase)) / math.sqrt(count)


def window_columns(col_count):
    first = col_count // 2 - MAIN // 2
    middle = np.arange(first, first + MAIN)
    before = np.arange(first - SIDE, first)
    after = np.arange(first + MAIN, first + MAIN + SIDE)
    return np.concatenate([middle, before, after])


def ramp_table(col_count, scale):
    grid = np.arange(col_count)
    columns = window_columns(col_count)
    offset = grid[:, None] - columns[None, :]
    odd = offset % 2 != 0
    safe = np.where(odd, offset, 1)
    table = np.where(offset == 0, 0.25, np.where(odd, -1.0 / (math.pi * safe) ** 2, 0.0)) * scale
    return np.pad(table, ((0, 0), (0, 2 * MAIN - columns.size)))


def split(value):
    high = value.astype(bf16)
    return high, (value - high.astype(f32)).astype(bf16)


def dot3(left, right):
    dot = functools.partial(jnp.dot, preferred_element_type=f32)
    return dot(left[0], right[0]) + (dot(left[0], right[1]) + dot(left[1], right[0]))


def each(start, stop, body):
    if stop - start <= 16:
        for i in range(start, stop):
            body(i)
    else:

        def step(i, carry):
            body(i)
            return carry

        lax.fori_loop(start, stop, step, 0)


def exchange_kernel(
    plan, x_any, h_any, k_any, row_any, col_any, sino, x, h, k, row, col, ah, al, bh, bl, window,
    pack, load_sem, own_sem, send_sem, recv_sem, pass_sem, land_sem,
):
    wide_count, depth, starts = plan
    rows = x.shape[0]
    block = 128
    mesh_ids = pl.DeviceIdType.MESH
    wide_pos, narrow_pos = lax.axis_index("wide"), lax.axis_index("narrow")
    other = 1 - narrow_pos
    moves = ((h_any, h), (x_any.at[0], x), (row_any, row), (col_any, col), (k_any, k))
    loads = [
        pltpu.make_async_copy(source, target, load_sem.at[i])
        for i, (source, target) in enumerate(moves)
    ]
    for load in loads:
        load.start()

    def greet(offset):
        target = lax.rem(wide_pos + offset, wide_count)
        pl.semaphore_signal(barrier, inc=1, device_id={"wide": target}, device_id_type=mesh_ids)

    barrier = pltpu.get_barrier_semaphore()
    each(1, wide_count, greet)
    pl.semaphore_signal(barrier, inc=1, device_id={"narrow": other}, device_id_type=mesh_ids)

    def part_of(step):
        return pl.ds(pl.multiple_of(step * block, block), block)

    def columns_first(step, carry):
        own = part_of(step)
        ah[own, :], al[own, :] = split(dot3(split(x[own, :]), (h[0], h[1])))
        return carry

    def damp(step, carry):
        own = part_of(step)
        part = dot3((h[0, own, :], h[1, own, :]), (ah[...], al[...]))
        part = part / (jnp.concatenate([row[own, :]] * (part.shape[1] // 128), axis=1) + col[...])
        bh[own, :], bl[own, :] = split(dot3(split(part), (h[0], h[1])))
        return carry

    def ramp(step, carry):
        own = part_of(step)
        part = dot3((h[0, own, :], h[1, own, :]), (bh[...], bl[...]))
        window[own, :] = dot3(split(jnp.log(part)), (k[0], k[1]))
        return carry

    loads[0].wait()
    loads[1].wait()
    lax.fori_loop(0, rows // block, columns_first, 0)
    for load in loads[2:]:
        load.wait()
    lax.fori_loop(0, rows // block, damp, 0)
    lax.fori_loop(0, rows // block, ramp, 0)
    for w, start in enumerate(starts):
        pack[w, :depth, :] = window[start : start + depth, :MAIN]
        sides = [
            window[start + 16 * j : start + 16 * j + 16, MAIN : MAIN + 2 * SIDE]
            for j in range(depth // 16)
        ]
        pack[w, depth:, : depth] = jnp.concatenate(sides, axis=1)
        pack[w, depth:, depth:] = jnp.zeros((16, MAIN - depth), f32)

    pl.semaphore_wait(barrier, wide_count)

    def offset_of(turn):
        return 1 + (turn + wide_count // 2 - 1) % (wide_count - 1)

    def send(turn):
        offset = offset_of(turn)
        target = lax.rem(wide_pos + offset, wide_count)
        pltpu.make_async_remote_copy(
            src_ref=pack.at[target],
            dst_ref=sino.at[wide_pos * 2 + narrow_pos],
            send_sem=send_sem.at[offset],
            recv_sem=recv_sem.at[offset],
            device_id={"wide": target},
            device_id_type=mesh_ids,
        ).start()

    def arrival(offset):
        source = lax.rem(wide_pos + wide_count - offset, wide_count)
        target = lax.rem(wide_pos + offset, wide_count)
        return pltpu.make_async_remote_copy(
            src_ref=pack.at[target],
            dst_ref=sino.at[source * 2 + narrow_pos],
            send_sem=send_sem.at[offset],
            recv_sem=recv_sem.at[offset],
            device_id={"wide": target},
            device_id_type=mesh_ids,
        )

    def hand_on(offset, side):
        source = lax.rem(wide_pos + wide_count - offset, wide_count)
        return pltpu.make_async_remote_copy(
            src_ref=sino.at[source * 2 + narrow_pos],
            dst_ref=sino.at[source * 2 + side],
            send_sem=pass_sem.at[offset],
            recv_sem=land_sem.at[offset],
            device_id={"narrow": other},
            device_id_type=mesh_ids,
        )

    each(0, wide_count - 1, send)
    own_copy = pltpu.make_async_copy(
        pack.at[wide_pos], sino.at[wide_pos * 2 + narrow_pos], own_sem
    )
    own_copy.start()
    own_copy.wait()
    hand_on(0, narrow_pos).start()

    def forward(turn):
        offset = offset_of(wide_count - 2 - turn)
        arrival(offset).wait_recv()
        hand_on(offset, narrow_pos).start()

    def finish(turn):
        offset = offset_of(wide_count - 2 - turn)
        arrival(offset).wait_send()
        hand_on(offset, narrow_pos).wait_send()
        hand_on(offset, other).wait_recv()

    each(0, wide_count - 1, forward)
    hand_on(0, narrow_pos).wait_send()
    hand_on(0, other).wait_recv()
    each(0, wide_count - 1, finish)


def exchanged(projection, total, wide_count, depth, starts):
    rows, cols = projection.shape[1:]
    hartley = np.stack(halves(hartley_table(rows)))
    ramp = np.stack(halves(ramp_table(cols, -math.pi / (attenuation * total))))
    row_part = 1.0 + paganin_strength * 4.0 * np.sin(np.pi * np.arange(rows) / rows) ** 2
    col_part = paganin_strength * 4.0 * np.sin(np.pi * np.arange(cols) / cols) ** 2
    row_part = np.repeat(row_part[:, None].astype(np.float32), 128, axis=1)
    col_part = col_part[None, :].astype(np.float32)
    anywhere = pl.BlockSpec(memory_space=pl.ANY)
    dma = pltpu.SemaphoreType.DMA
    return pl.pallas_call(
        functools.partial(exchange_kernel, (wide_count, depth, starts)),
        out_shape=jax.ShapeDtypeStruct((total, depth + 16, MAIN), f32),
        in_specs=[anywhere] * 5,
        out_specs=pl.BlockSpec(memory_space=pltpu.VMEM),
        scratch_shapes=[
            pltpu.VMEM((rows, cols), f32),
            pltpu.VMEM(hartley.shape, bf16),
            pltpu.VMEM(ramp.shape, bf16),
            pltpu.VMEM(row_part.shape, f32),
            pltpu.VMEM(col_part.shape, f32),
        ]
        + [pltpu.VMEM((rows, cols), bf16)] * 4
        + [
            pltpu.VMEM((rows, 2 * MAIN), f32),
            pltpu.VMEM((wide_count, depth + 16, MAIN), f32),
            dma((5,)),
            dma,
        ]
        + [dma((wide_count,))] * 4,
        compiler_params=pltpu.CompilerParams(
            vmem_limit_bytes=60 * 2**20, collective_id=0, has_side_effects=True
        ),
        name="filter_exchange",
    )(
        projection,
        jnp.asarray(hartley),
        jnp.asarray(ramp),
        jnp.asarray(row_part),
        jnp.asarray(col_part),
    )


def conduct(diff):
    base = 1.0 + diff * diff * (1.0 / contrast**2)
    guess = pl.reciprocal(base, approx=True)
    return diff * (guess * (2.0 - base * guess))


def volume_kernel(plan, ang_ref, cos_ref, sin_ref, sino_ref, out_ref, f2, wh0, wl0, wh1, wl1, u):
    slab, tile_y, local_y, z_start, wide_count = plan
    total, depth = sino_ref.shape[0], sino_ref.shape[1] - 16
    wide_pos, narrow_pos = lax.axis_index("wide"), lax.axis_index("narrow")
    y_skip = tile_y - (local_y - tile_y)
    y_first = narrow_pos * y_skip
    x_row = lax.broadcasted_iota(jnp.int32, (16, XV), 1).astype(f32) + (0.5 - 0.5 * XV)
    lanes16 = lax.broadcasted_iota(jnp.int32, (16, XV), 0)
    middle = [(lanes16 + (SIDE + 16 * j)).astype(f32).astype(bf16) for j in range(MAIN // 16)]
    outer = jnp.where(lanes16 < SIDE, lanes16, lanes16 + MAIN).astype(f32).astype(bf16)
    cells = middle + [outer]
    centre = 0.5 * MAIN + SIDE - 0.5

    def weights(group, pair, high_ref, low_ref):
        for side in range(2):
            own = slice(side * XV, (side + 1) * XV)
            y_pos = (y_first + 2 * pair + side).astype(f32) + (0.5 - 0.5 * YV)
            for a in range(GROUP):
                number = ang_ref[group * GROUP + a]
                place = x_row * cos_ref[number] + (y_pos * sin_ref[number] + centre)
                lower = jnp.floor(place)
                frac = place - lower
                coarse = jnp.floor(frac * 256.0 + 0.5) * (1.0 / 256.0)
                fine = frac - coarse
                here, there = lower.astype(bf16), (lower + 1.0).astype(bf16)
                left, right = (1.0 - coarse).astype(bf16), coarse.astype(bf16)
                left_fine, right_fine = (-fine).astype(bf16), fine.astype(bf16)
                zero = jnp.zeros_like(left)
                for j, cell in enumerate(cells):
                    row = a * MAIN + j * 16 if j < len(middle) else GROUP * MAIN + a * 16
                    is_here, is_there = cell == here, cell == there
                    high_ref[row : row + 16, own] = jnp.where(
                        is_here, left, jnp.where(is_there, right, zero)
                    )
                    low_ref[row : row + 16, own] = jnp.where(
                        is_here, left_fine, jnp.where(is_there, right_fine, zero)
                    )

    def project(group, pair, high_ref, low_ref):
        both = jnp.dot(f2[...], high_ref[...], preferred_element_type=f32)
        rest = jnp.dot(f2[:depth, :], low_ref[...], preferred_element_type=f32)
        value = both[:depth] + (both[depth:] + rest)
        for side in range(2):
            own = value[:, side * XV : (side + 1) * XV]
            if total > GROUP:
                own = own + jnp.where(group > 0, u[2 * pair + side], 0.0)
            u[2 * pair + side] = own

    def one_group(group, carry):
        for a in range(GROUP):
            high, low = split(sino_ref[group * GROUP + a, :depth, :])
            f2[:depth, a * MAIN : (a + 1) * MAIN] = high
            f2[depth:, a * MAIN : (a + 1) * MAIN] = low
        for j in range(depth // 16):
            parts = [
                sino_ref[group * GROUP + a, depth:, 16 * j : 16 * j + 16] for a in range(GROUP)
            ]
            high, low = split(jnp.concatenate(parts, axis=1))
            f2[16 * j : 16 * j + 16, GROUP * MAIN :] = high
            f2[depth + 16 * j : depth + 16 * j + 16, GROUP * MAIN :] = low
        weights(group, jnp.int32(0), wh0, wl0)

        def two_pairs(step, inner):
            weights(group, 2 * step + 1, wh1, wl1)
            project(group, 2 * step, wh0, wl0)
            weights(group, 2 * step + 2, wh0, wl0)
            project(group, 2 * step + 1, wh1, wl1)
            return inner

        lax.fori_loop(0, local_y // 4, two_pairs, 0)
        return carry

    if total > GROUP:
        lax.fori_loop(0, total // GROUP, one_group, 0)
    else:
        one_group(0, 0)

    z_ids = lax.broadcasted_iota(jnp.int32, (depth, XV), 0)
    x_ids = lax.broadcasted_iota(jnp.int32, (depth, XV), 1)
    has_z = z_ids < depth - 1
    has_x = x_ids < XV - 1

    def row_step(y, carry):
        now, flux_before = carry
        later = u[jnp.minimum(y + 1, local_y - 1)]
        flux_y = conduct(later - now)
        flux_z = conduct(jnp.where(has_z, pltpu.roll(now, depth - 1, 0) - now, 0.0))
        flux_x = conduct(jnp.where(has_x, pltpu.roll(now, XV - 1, 1) - now, 0.0))
        update = (flux_y - flux_before) + (flux_z - pltpu.roll(flux_z, 1, 0))
        update = update + (flux_x - pltpu.roll(flux_x, 1, 1))
        u[y] = now + time_step * update
        return later, flux_y

    for step in range(STEPS):
        lax.fori_loop(0, local_y, row_step, (u[0], jnp.zeros((depth, XV), f32)), unroll=2)

    z_skip = wide_pos * slab - z_start(wide_pos)
    if slab % 8 == 0:
        z_skip = pl.multiple_of(z_skip, 8)
    y_own = narrow_pos * (local_y - tile_y)
    for y in range(tile_y):
        out_ref[:, y, :] = u[y_own + y, pl.ds(z_skip, slab), :]


def shards(projections, angle_index):
    wide_count = lax.axis_size("wide")
    narrow_count = lax.axis_size("narrow")
    rows = projections.shape[1]
    total = angle_index.shape[0]
    slab = rows // wide_count
    depth = -(-(slab + 12) // 16) * 16
    tile_y = YV // narrow_count
    local_y = tile_y + STEPS

    def z_start(wide_pos):
        first = (wide_pos * slab + 8 - STEPS) // 8 * 8 - 8
        if isinstance(wide_pos, int):
            return min(max(first, 0), rows - depth)
        return jnp.minimum(jnp.maximum(first, 0), rows - depth)

    starts = [z_start(w) for w in range(wide_count)]
    sino = exchanged(projections, total, wide_count, depth, starts)
    angles = np.arange(total) * (math.pi / total)
    vmem = pl.BlockSpec(memory_space=pltpu.VMEM)
    smem = pl.BlockSpec(memory_space=pltpu.SMEM)
    inner = GROUP * (MAIN + 2 * SIDE)
    return pl.pallas_call(
        functools.partial(volume_kernel, (slab, tile_y, local_y, z_start, wide_count)),
        out_shape=jax.ShapeDtypeStruct((slab, tile_y, XV), f32),
        in_specs=[smem, smem, smem, vmem],
        out_specs=vmem,
        scratch_shapes=[pltpu.VMEM((2 * depth, inner), bf16)]
        + [pltpu.VMEM((inner, 2 * XV), bf16)] * 4
        + [pltpu.VMEM((local_y, depth, XV), f32)],
        compiler_params=pltpu.CompilerParams(vmem_limit_bytes=60 * 2**20),
        name="volume",
    )(
        angle_index,
        jnp.asarray(np.cos(angles).astype(np.float32)),
        jnp.asarray(np.sin(angles).astype(np.float32)),
        sino,
    )


def solution(mesh):
    return jax.shard_map(
        shards,
        mesh=mesh,
        in_specs=(P(("scan", "wide", "narrow"), None, None), P("scan")),
        out_specs=P(("scan", "wide"), "narrow", None),
        check_vma=False,
    )
```

```python
import functools
import math

import jax
import jax.numpy as jnp
import ml_dtypes
import numpy as np
from jax import lax
from jax.experimental import pallas as pl
from jax.experimental.pallas import tpu as pltpu
from jax.sharding import PartitionSpec as P

XV = 128
YV = 64
STEPS = 4
GROUP = 16
MAIN = 128
SIDE = 8

paganin_strength = 0.25
attenuation = 0.01
contrast = 0.8
time_step = 0.15
bf16 = jnp.bfloat16
f32 = jnp.float32


def halves(table):
    high = table.astype(ml_dtypes.bfloat16)
    low = (table - high.astype(np.float64)).astype(ml_dtypes.bfloat16)
    return high, low


def hartley_table(count):
    grid = np.arange(count)
    phase = (grid[:, None] * grid[None, :] % count) * (2.0 * math.pi / count)
    return (np.cos(phase) + np.sin(phase)) / math.sqrt(count)


def window_columns(col_count):
    first = col_count // 2 - MAIN // 2
    middle = np.arange(first, first + MAIN)
    before = np.arange(first - SIDE, first)
    after = np.arange(first + MAIN, first + MAIN + SIDE)
    return np.concatenate([middle, before, after])


def ramp_table(col_count, scale):
    grid = np.arange(col_count)
    columns = window_columns(col_count)
    offset = grid[:, None] - columns[None, :]
    odd = offset % 2 != 0
    safe = np.where(odd, offset, 1)
    table = np.where(offset == 0, 0.25, np.where(odd, -1.0 / (math.pi * safe) ** 2, 0.0)) * scale
    return np.pad(table, ((0, 0), (0, 2 * MAIN - columns.size)))


def split(value):
    high = value.astype(bf16)
    return high, (value - high.astype(f32)).astype(bf16)


def stacked(value):
    high = value.astype(bf16).astype(f32)
    return jnp.concatenate([high, value - high], axis=0).astype(bf16)


def dot3(left, right):
    dot = functools.partial(jnp.dot, preferred_element_type=f32)
    return dot(left[0], right[0]) + (dot(left[0], right[1]) + dot(left[1], right[0]))


def each(start, stop, body):
    if stop - start <= 16:
        for i in range(start, stop):
            body(i)
    else:

        def step(i, carry):
            body(i)
            return carry

        lax.fori_loop(start, stop, step, 0)


def exchange_kernel(
    plan, x_any, h_any, k_any, row_any, col_any, sino, x, h, k, row, col, ah, al, bh, bl, window,
    pack, load_sem, own_sem, send_sem, recv_sem, pass_sem, land_sem,
):
    wide_count, depth, starts = plan
    rows = x.shape[0]
    block = 128
    mesh_ids = pl.DeviceIdType.MESH
    wide_pos, narrow_pos = lax.axis_index("wide"), lax.axis_index("narrow")
    other = 1 - narrow_pos
    moves = ((h_any, h), (x_any.at[0], x), (row_any, row), (col_any, col), (k_any, k))
    loads = [
        pltpu.make_async_copy(source, target, load_sem.at[i])
        for i, (source, target) in enumerate(moves)
    ]
    for load in loads:
        load.start()

    def greet(offset):
        target = lax.rem(wide_pos + offset, wide_count)
        pl.semaphore_signal(barrier, inc=1, device_id={"wide": target}, device_id_type=mesh_ids)

    barrier = pltpu.get_barrier_semaphore()
    each(1, wide_count, greet)
    pl.semaphore_signal(barrier, inc=1, device_id={"narrow": other}, device_id_type=mesh_ids)

    def part_of(step):
        return pl.ds(pl.multiple_of(step * block, block), block)

    def columns_first(step, carry):
        own = part_of(step)
        ah[own, :], al[own, :] = split(dot3(split(x[own, :]), (h[0], h[1])))
        return carry

    def damp(step, carry):
        own = part_of(step)
        part = dot3((h[0, own, :], h[1, own, :]), (ah[...], al[...]))
        part = part / (jnp.concatenate([row[own, :]] * (part.shape[1] // 128), axis=1) + col[...])
        bh[own, :], bl[own, :] = split(dot3(split(part), (h[0], h[1])))
        return carry

    def ramp(step, carry):
        own = part_of(step)
        part = dot3((h[0, own, :], h[1, own, :]), (bh[...], bl[...]))
        window[own, :] = dot3(split(jnp.log(part)), (k[0], k[1]))
        return carry

    loads[0].wait()
    loads[1].wait()
    lax.fori_loop(0, rows // block, columns_first, 0)
    for load in loads[2:]:
        load.wait()
    lax.fori_loop(0, rows // block, damp, 0)
    lax.fori_loop(0, rows // block, ramp, 0)
    for w, start in enumerate(starts):
        pack[w, :depth, :] = window[start : start + depth, :MAIN]
        sides = [
            window[start + j : start + min(j + 16, depth), MAIN : MAIN + 2 * SIDE]
            for j in range(0, depth, 16)
        ]
        if depth % 16:
            sides[-1] = jnp.concatenate([sides[-1], jnp.zeros((8, 2 * SIDE), f32)], axis=0)
        sides.append(jnp.zeros((16, MAIN - 16 * len(sides)), f32))
        pack[w, depth:, :] = jnp.concatenate(sides, axis=1)

    pl.semaphore_wait(barrier, wide_count)

    def offset_of(turn):
        return 1 + (turn + wide_count // 2 - 1) % (wide_count - 1)

    def send(turn):
        offset = offset_of(turn)
        target = lax.rem(wide_pos + offset, wide_count)
        pltpu.make_async_remote_copy(
            src_ref=pack.at[target],
            dst_ref=sino.at[wide_pos * 2 + narrow_pos],
            send_sem=send_sem.at[offset],
            recv_sem=recv_sem.at[offset],
            device_id={"wide": target},
            device_id_type=mesh_ids,
        ).start()

    def arrival(offset):
        source = lax.rem(wide_pos + wide_count - offset, wide_count)
        target = lax.rem(wide_pos + offset, wide_count)
        return pltpu.make_async_remote_copy(
            src_ref=pack.at[target],
            dst_ref=sino.at[source * 2 + narrow_pos],
            send_sem=send_sem.at[offset],
            recv_sem=recv_sem.at[offset],
            device_id={"wide": target},
            device_id_type=mesh_ids,
        )

    def hand_on(offset, side):
        source = lax.rem(wide_pos + wide_count - offset, wide_count)
        return pltpu.make_async_remote_copy(
            src_ref=sino.at[source * 2 + narrow_pos],
            dst_ref=sino.at[source * 2 + side],
            send_sem=pass_sem.at[offset],
            recv_sem=land_sem.at[offset],
            device_id={"narrow": other},
            device_id_type=mesh_ids,
        )

    each(0, wide_count - 1, send)
    own_copy = pltpu.make_async_copy(
        pack.at[wide_pos], sino.at[wide_pos * 2 + narrow_pos], own_sem
    )
    own_copy.start()
    own_copy.wait()
    hand_on(0, narrow_pos).start()

    def forward(turn):
        offset = offset_of(wide_count - 2 - turn)
        arrival(offset).wait_recv()
        hand_on(offset, narrow_pos).start()

    def finish(turn):
        offset = offset_of(wide_count - 2 - turn)
        arrival(offset).wait_send()
        hand_on(offset, narrow_pos).wait_send()
        hand_on(offset, other).wait_recv()

    each(0, wide_count - 1, forward)
    hand_on(0, narrow_pos).wait_send()
    hand_on(0, other).wait_recv()
    each(0, wide_count - 1, finish)


def exchanged(projection, total, wide_count, depth, starts):
    rows, cols = projection.shape[1:]
    hartley = np.stack(halves(hartley_table(rows)))
    ramp = np.stack(halves(ramp_table(cols, -math.pi / (attenuation * total * contrast))))
    row_part = 1.0 + paganin_strength * 4.0 * np.sin(np.pi * np.arange(rows) / rows) ** 2
    col_part = paganin_strength * 4.0 * np.sin(np.pi * np.arange(cols) / cols) ** 2
    row_part = np.repeat(row_part[:, None].astype(np.float32), 128, axis=1)
    col_part = col_part[None, :].astype(np.float32)
    anywhere = pl.BlockSpec(memory_space=pl.ANY)
    dma = pltpu.SemaphoreType.DMA
    return pl.pallas_call(
        functools.partial(exchange_kernel, (wide_count, depth, starts)),
        out_shape=jax.ShapeDtypeStruct((total, depth + 16, MAIN), f32),
        in_specs=[anywhere] * 5,
        out_specs=pl.BlockSpec(memory_space=pltpu.VMEM),
        scratch_shapes=[
            pltpu.VMEM((rows, cols), f32),
            pltpu.VMEM(hartley.shape, bf16),
            pltpu.VMEM(ramp.shape, bf16),
            pltpu.VMEM(row_part.shape, f32),
            pltpu.VMEM(col_part.shape, f32),
        ]
        + [pltpu.VMEM((rows, cols), bf16)] * 4
        + [
            pltpu.VMEM((rows, 2 * MAIN), f32),
            pltpu.VMEM((wide_count, depth + 16, MAIN), f32),
            dma((5,)),
            dma,
        ]
        + [dma((wide_count,))] * 4,
        compiler_params=pltpu.CompilerParams(
            vmem_limit_bytes=60 * 2**20, collective_id=0, has_side_effects=True
        ),
        name="filter_exchange",
    )(
        projection,
        jnp.asarray(hartley),
        jnp.asarray(ramp),
        jnp.asarray(row_part),
        jnp.asarray(col_part),
    )


def conduct(diff):
    return diff * pl.reciprocal(1.0 + diff * diff, approx=True)


def volume_kernel(plan, ang_ref, cos_ref, sin_ref, sino_ref, out_ref, f2, wh0, wl0, wh1, wl1, u):
    slab, tile_y, local_y, z_start, wide_count = plan
    total, depth = sino_ref.shape[0], sino_ref.shape[1] - 16
    depth16 = -(-depth // 16) * 16
    wide_pos, narrow_pos = lax.axis_index("wide"), lax.axis_index("narrow")
    y_skip = tile_y - (local_y - tile_y)
    y_first = narrow_pos * y_skip
    x_row = lax.broadcasted_iota(jnp.int32, (16, XV), 1).astype(f32) + (0.5 - 0.5 * XV)
    lanes16 = lax.broadcasted_iota(jnp.int32, (16, XV), 0)
    middle = [(lanes16 + (SIDE + 16 * j)).astype(f32).astype(bf16) for j in range(MAIN // 16)]
    outer = jnp.where(lanes16 < SIDE, lanes16, lanes16 + MAIN).astype(f32).astype(bf16)
    cells = middle + [outer]
    centre = 0.5 * MAIN + SIDE - 0.5

    def weights(group, pair, high_ref, low_ref, angles):
        for side in range(2):
            own = slice(side * XV, (side + 1) * XV)
            y_pos = (y_first + 2 * pair + side).astype(f32) + (0.5 - 0.5 * YV)
            for a in angles:
                number = ang_ref[group * GROUP + a]
                place = x_row * cos_ref[number] + (y_pos * sin_ref[number] + centre)
                lower = jnp.floor(place)
                frac = place - lower
                coarse = jnp.floor(frac * 256.0 + 0.5) * (1.0 / 256.0)
                fine = frac - coarse
                here, there = lower.astype(bf16), (lower + 1.0).astype(bf16)
                left, right = (1.0 - coarse).astype(bf16), coarse.astype(bf16)
                left_fine, right_fine = (-fine).astype(bf16), fine.astype(bf16)
                zero = jnp.zeros_like(left)
                for j, cell in enumerate(cells):
                    row = a * MAIN + j * 16 if j < len(middle) else GROUP * MAIN + a * 16
                    is_here, is_there = cell == here, cell == there
                    high_ref[row : row + 16, own] = jnp.where(
                        is_here, left, jnp.where(is_there, right, zero)
                    )
                    low_ref[row : row + 16, own] = jnp.where(
                        is_here, left_fine, jnp.where(is_there, right_fine, zero)
                    )

    def project(group, pair, now_refs, later_refs):
        both, rest = 0.0, 0.0
        for part in range(GROUP * (MAIN + 2 * SIDE) // 256):
            own = slice(256 * part, 256 * part + 256)
            both = both + jnp.dot(f2[:, own], now_refs[0][own, :], preferred_element_type=f32)
            rest = rest + jnp.dot(
                f2[:depth16, own], now_refs[1][own, :], preferred_element_type=f32
            )
            if 2 * part < GROUP:
                weights(group, pair + 1, *later_refs, (2 * part, 2 * part + 1))
        value = both[:depth] + (both[depth:] + rest[:depth])
        for side in range(2):
            own = value[:, side * XV : (side + 1) * XV]
            if total > GROUP:
                own = own + jnp.where(group > 0, u[2 * pair + side], 0.0)
            u[2 * pair + side] = own

    def one_group(group, carry):
        for a in range(GROUP):
            own = sino_ref[group * GROUP + a, :depth, :]
            f2[:, a * MAIN : (a + 1) * MAIN] = stacked(own)
        sides = [
            jnp.concatenate(
                [sino_ref[group * GROUP + a, depth:, j : j + 16] for a in range(GROUP)], axis=1
            )
            for j in range(0, depth, 16)
        ]
        f2[:, GROUP * MAIN :] = stacked(jnp.concatenate(sides, axis=0)[:depth])
        even, odd = (wh0, wl0), (wh1, wl1)
        weights(group, jnp.int32(0), *even, range(GROUP))

        def two_pairs(step, inner):
            project(group, 2 * step, even, odd)
            project(group, 2 * step + 1, odd, even)
            return inner

        lax.fori_loop(0, local_y // 4, two_pairs, 0)
        return carry

    if total > GROUP:
        lax.fori_loop(0, total // GROUP, one_group, 0)
    else:
        one_group(0, 0)

    z_ids = lax.broadcasted_iota(jnp.int32, (depth, XV), 0)
    x_ids = lax.broadcasted_iota(jnp.int32, (depth, XV), 1)
    has_z = z_ids < depth - 1
    has_x = x_ids < XV - 1

    def row_step(y, carry):
        now, flux_before = carry
        later = u[jnp.minimum(y + 1, local_y - 1)]
        flux_y = conduct(later - now)
        flux_z = conduct(jnp.where(has_z, pltpu.roll(now, depth - 1, 0) - now, 0.0))
        flux_x = conduct(jnp.where(has_x, pltpu.roll(now, XV - 1, 1) - now, 0.0))
        update = (flux_y - flux_before) + (flux_z - pltpu.roll(flux_z, 1, 0))
        update = update + (flux_x - pltpu.roll(flux_x, 1, 1))
        u[y] = now + time_step * update
        return later, flux_y

    for step in range(STEPS):
        lax.fori_loop(0, local_y, row_step, (u[0], jnp.zeros((depth, XV), f32)), unroll=12)

    z_skip = wide_pos * slab - z_start(wide_pos)
    y_own = narrow_pos * (local_y - tile_y)
    for y in range(tile_y):
        out_ref[:, y, :] = u[y_own + y, pl.ds(z_skip, slab), :] * contrast


def shards(projections, angle_index):
    wide_count = lax.axis_size("wide")
    narrow_count = lax.axis_size("narrow")
    rows = projections.shape[1]
    total = angle_index.shape[0]
    slab = rows // wide_count
    depth = -(-(slab + 2 * STEPS) // 8) * 8
    tile_y = YV // narrow_count
    local_y = tile_y + STEPS

    def z_start(wide_pos):
        first = wide_pos * slab - STEPS
        if isinstance(wide_pos, int):
            return min(max(first, 0), rows - depth)
        return jnp.minimum(jnp.maximum(first, 0), rows - depth)

    starts = [z_start(w) for w in range(wide_count)]
    sino = exchanged(projections, total, wide_count, depth, starts)
    angles = np.arange(total) * (math.pi / total)
    vmem = pl.BlockSpec(memory_space=pltpu.VMEM)
    smem = pl.BlockSpec(memory_space=pltpu.SMEM)
    inner = GROUP * (MAIN + 2 * SIDE)
    return pl.pallas_call(
        functools.partial(volume_kernel, (slab, tile_y, local_y, z_start, wide_count)),
        out_shape=jax.ShapeDtypeStruct((slab, tile_y, XV), f32),
        in_specs=[smem, smem, smem, vmem],
        out_specs=vmem,
        scratch_shapes=[pltpu.VMEM((2 * depth, inner), bf16)]
        + [pltpu.VMEM((inner, 2 * XV), bf16)] * 4
        + [pltpu.VMEM((local_y, depth, XV), f32)],
        compiler_params=pltpu.CompilerParams(vmem_limit_bytes=60 * 2**20),
        name="volume",
    )(
        angle_index,
        jnp.asarray(np.cos(angles).astype(np.float32)),
        jnp.asarray(np.sin(angles).astype(np.float32)),
        sino,
    )


def solution(mesh):
    return jax.shard_map(
        shards,
        mesh=mesh,
        in_specs=(P(("scan", "wide", "narrow"), None, None), P("scan")),
        out_specs=P(("scan", "wide"), "narrow", None),
        check_vma=False,
    )
```
